32 devices in a mesh: row: 4 (over z), col: 8 (over y, x, core).
Axes of the slice: x: 2, y: 2, z: 4, core: 2. Of those that a mesh axis runs over, the one named last changes fastest.
Arguments:
- tokens: bfloat16 [1024, 2048], P(('row', 'col')), may hold values from -6 to 6
- routes: int32 [1024, 6], P(('row', 'col')), may hold values from 0 to 63, as said below
- router: bfloat16 [2048, 64], replicated, may hold values from -0.125 to 0.125
- w_in: bfloat16 [128, 2048, 1408], P(('row', 'col')), may hold values from -0.125 to 0.125
- w_out: bfloat16 [128, 704, 2048], P(('row', 'col')), may hold values from -0.15625 to 0.15625
- cache_prefill: bfloat16 [2304, 9216], P(('row', 'col')), may hold values from -6 to 6
- page_slot: int32 [2304], P(('row', 'col')), may hold values from 0 to 2303, as said below
Outputs:
- moe_out: bfloat16 [1024, 2048], P(('row', 'col'))
- cache_decode: bfloat16 [2304, 9216], P(('row', 'col'))
The draws below stay inside these ranges and needn't reach their ends.
Inputs may be any that keep to these rules, and one draw needn't show every extreme that they name: `routes`: each row names 6 different experts. In the rows of one device no expert is named more than 6 times, and one expert, the same for all devices, is named exactly 6 times in every device's rows. `page_slot`: A permutation of the page rows. Every device receives exactly 72 pages; at most 3 pages go from one device to one device, and some pair of devices reaches 3.
All inputs are finite; a program needn't handle non-finite values.
Results may differ from the reference program's by a relative error of at most 0.0065.
Values may be sent and summed in bfloat16 or wider, within the bound.
A program may use at most 128 MiB of HBM per device.

```python
import jax
import jax.numpy as jnp
from jax import lax

D = 2048
FF = 1408
EXPERTS = 64
TOP = 6
TOK_DEV = 32
PAGE = 16
FFH = 704
KVW = 576
TOKENS = 1024
CAPE = 6
PAGES_DEV = 72
CPAGES = 2304
N_ROW = 4
N_COL = 8


def draw_routes(key, part):
    hot_expert = jax.random.randint(jax.random.fold_in(key, 11), (), 0, EXPERTS).astype(jnp.int32)
    block_count = TOKENS // TOK_DEV
    spare_count = TOP * TOK_DEV - CAPE

    def one_block(block_id):
        block_key = jax.random.fold_in(jax.random.fold_in(key, 12), block_id)
        first_key, second_key, third_key = jax.random.split(block_key, 3)
        others = (jnp.arange(EXPERTS - 1, dtype=jnp.int32) + hot_expert + 1) % EXPERTS
        candidates = jnp.repeat(others, CAPE, total_repeat_length=(EXPERTS - 1) * CAPE)
        chosen = jnp.sort(jax.random.permutation(first_key, (EXPERTS - 1) * CAPE)[:spare_count])
        sequence = jnp.concatenate([jnp.full((CAPE,), hot_expert, jnp.int32), candidates[chosen]])
        layout = sequence.reshape(TOP, TOK_DEV).T
        layout = layout[jax.random.permutation(second_key, TOK_DEV)]
        row_keys = jax.random.split(third_key, TOK_DEV)
        return jax.vmap(jax.random.permutation)(row_keys, layout)
    return jax.vmap(one_block)(jnp.arange(block_count)).reshape(TOKENS, TOP).astype(jnp.int32)


def draw_page_slot(key, part):
    device_count = CPAGES // PAGES_DEV
    base_share = PAGES_DEV // device_count
    extra_count = PAGES_DEV % device_count
    keys_four = jax.random.split(jax.random.fold_in(key, 21), 4)
    ranked = jax.random.permutation(keys_four[0], device_count)
    counts = base_share + (ranked < extra_count).astype(jnp.int32)
    run_ends = jnp.cumsum(counts)
    offsets = jnp.sum((run_ends[None, :] <= jnp.arange(PAGES_DEV)[:, None]).astype(jnp.int32), axis=1)
    base_shift = jax.random.permutation(keys_four[1], device_count)
    orders = jax.vmap(lambda number: jax.random.permutation(jax.random.fold_in(keys_four[2], number), PAGES_DEV))(jnp.arange(device_count))
    target = (base_shift[:, None] + offsets[orders]) % device_count
    within = jax.vmap(lambda number: jax.random.permutation(jax.random.fold_in(keys_four[3], number), PAGES_DEV))(jnp.arange(device_count))
    landing = within[target, orders]
    return (target * PAGES_DEV + landing).reshape(-1).astype(jnp.int32)


def levels(stream_key, extent, cuts, low, largest):
    factor_of = 1.0
    for position, blocks in cuts:
        draws = jax.random.uniform(jax.random.fold_in(jax.random.fold_in(stream_key, 6), position), (blocks,), jnp.float32, low / len(cuts), largest / len(cuts))
        factor_of = factor_of * jnp.repeat(jnp.exp(draws), extent[position] // blocks).reshape((-1,) + (1,) * (len(extent) - 1 - position))
    return factor_of


def scatter_about(own_key, dims, deviation, limit, pieces=(), kind=jnp.bfloat16):
    result = deviation * jax.random.normal(own_key, dims, jnp.float32)
    if pieces:
        result = result * levels(own_key, dims, pieces, -0.22, 0.18)
    return jnp.clip(result, -limit, limit).astype(kind)


def setup_inputs(seed: int = 0) -> dict:
    keys = jax.random.split(jax.random.key(seed), 8)
    tokens = scatter_about(keys[0], (TOKENS, D), 1.0, 6.0, ((0, 32),))
    routes = draw_routes(jax.random.fold_in(keys[7], 71), 0)
    router = scatter_about(keys[2], (D, EXPERTS), D ** -0.5, 0.125)
    w_in = scatter_about(keys[3], (2 * EXPERTS, D, 2 * FFH), D ** -0.5, 0.125, ((0, 32),))
    w_out = scatter_about(keys[4], (2 * EXPERTS, FFH, D), FF ** -0.5, 0.15625, ((0, 32),))
    cache_prefill = scatter_about(keys[5], (CPAGES, PAGE * KVW), 1.0, 6.0, ((0, 32),))
    page_slot = draw_page_slot(jax.random.fold_in(keys[7], 71), 0)
    return dict(tokens=tokens, routes=routes, router=router, w_in=w_in, w_out=w_out, cache_prefill=cache_prefill, page_slot=page_slot)


route_scale = 2.446


def gate_values_of(tokens, routes, router):
    logits = jnp.dot(tokens, router, preferred_element_type=jnp.float32)
    scores = jax.nn.sigmoid(logits)
    picked = jnp.take_along_axis(scores, routes, axis=1)
    return route_scale * picked / jnp.sum(picked, axis=1, keepdims=True)


def half_output(token_rows, w_first, w_second):
    gate_up = jnp.dot(token_rows, w_first, preferred_element_type=jnp.float32)
    hidden_width = w_second.shape[0]
    activated = (jax.nn.silu(gate_up[:, :hidden_width]) * gate_up[:, hidden_width:]).astype(jnp.bfloat16)
    return jnp.dot(activated, w_second, preferred_element_type=jnp.float32).astype(jnp.bfloat16)


def reference(tokens, routes, router, w_in, w_out, cache_prefill, page_slot):
    gate_values = gate_values_of(tokens, routes, router)
    flat_routes = routes.reshape(-1).astype(jnp.int32)
    ordering = jnp.argsort(flat_routes, stable=True).astype(jnp.int32)
    totals = jnp.zeros((EXPERTS,), jnp.int32).at[flat_routes].add(1)
    starts = (jnp.cumsum(totals) - totals).astype(jnp.int32)
    window_rows = CAPE * N_ROW * N_COL
    padded = jnp.concatenate([ordering, jnp.zeros((window_rows,), jnp.int32)])
    gate_flat = gate_values.reshape(-1)

    def one_expert(running, expert):
        offsets = jnp.arange(window_rows, dtype=jnp.int32)
        chosen = lax.dynamic_slice_in_dim(padded, starts[expert], window_rows)
        is_live = offsets < totals[expert]
        token_rows = tokens[chosen // TOP]
        part_low = half_output(token_rows, w_in[expert], w_out[expert])
        part_high = half_output(token_rows, w_in[EXPERTS + expert], w_out[EXPERTS + expert])
        merged = (part_low.astype(jnp.float32) + part_high.astype(jnp.float32)).astype(jnp.bfloat16)
        weight = jnp.where(is_live, gate_flat[chosen], jnp.zeros_like(gate_flat[chosen]))
        running = running.at[chosen // TOP].add(weight[:, None] * merged.astype(jnp.float32))
        return running, None

    summed, unused = lax.scan(one_expert, jnp.zeros((TOKENS, D), jnp.float32), jnp.arange(EXPERTS, dtype=jnp.int32))
    moe_out = summed.astype(jnp.bfloat16)
    cache_decode = jnp.zeros_like(cache_prefill).at[page_slot].set(cache_prefill)
    return (moe_out, cache_decode)
```

```python
import functools

import jax
import jax.numpy as jnp
from jax import lax
from jax.experimental import pallas as pl
from jax.experimental.pallas import tpu as pltpu
from jax.sharding import PartitionSpec as P

EXPERTS = 64
CAPE = 6
AXES = ("row", "col")
ROUTE_SCALE = 2.446
CHUNK = 512


def experts_kernel(base_ref, x_ref, router_ref, routes_ref, w_in_ref, w_out_ref, out_ref,
                   gates, ranks, weighted):
    step = pl.program_id(0)
    steps = pl.num_programs(0)
    count = x_ref.shape[0]
    rows = weighted.shape[1]
    hidden = w_out_ref.shape[1]

    @pl.when(step == 0)
    def _():
        expert_row = lax.broadcasted_iota(jnp.int32, (EXPERTS, CHUNK), 0)
        earlier = (
            lax.broadcasted_iota(jnp.int32, (CHUNK, CHUNK), 0)
            < lax.broadcasted_iota(jnp.int32, (CHUNK, CHUNK), 1)
        ).astype(jnp.float32).astype(jnp.bfloat16)
        offset = jnp.zeros((EXPERTS, 1), jnp.float32)
        for begin in range(0, count, CHUNK):
            part = slice(begin, begin + CHUNK)
            logits = lax.dot_general(
                router_ref[...], x_ref[part, :], (((1,), (1,)), ((), ())),
                preferred_element_type=jnp.float32,
            )
            scores = 1.0 / (1.0 + jnp.exp(-logits))
            named = jnp.zeros((EXPERTS, CHUNK), jnp.float32)
            for k in range(routes_ref.shape[0]):
                named = jnp.where(routes_ref[k : k + 1, part] == expert_row, 1.0, named)
            picked = scores * named
            gates[:, part] = ROUTE_SCALE * picked / jnp.sum(picked, axis=0, keepdims=True)
            before = offset + jnp.dot(
                named.astype(jnp.bfloat16), earlier, preferred_element_type=jnp.float32
            )
            ranks[:, part] = jnp.where(named > 0.0, before, -1.0)
            offset = offset + jnp.sum(named, axis=1, keepdims=True)

    expert = base_ref[0] + step

    def chosen(which, part):
        slots = lax.broadcasted_iota(jnp.int32, (rows, part.size), 0).astype(jnp.float32)
        return ranks[pl.ds(which, 1), part] == slots

    picked_rows = jnp.zeros((rows, x_ref.shape[1]), jnp.float32)
    row_gate = jnp.zeros((rows, 1), jnp.float32)
    for begin in range(0, count, CHUNK):
        part = pl.ds(begin, CHUNK)
        hit = chosen(expert, part)
        picked_rows += jnp.dot(
            hit.astype(jnp.float32).astype(jnp.bfloat16), x_ref[part, :],
            preferred_element_type=jnp.float32,
        )
        row_gate += jnp.sum(
            jnp.where(hit, gates[pl.ds(expert, 1), part], 0.0), axis=1, keepdims=True
        )
    gate_up = jnp.dot(
        picked_rows.astype(jnp.bfloat16), w_in_ref[0], preferred_element_type=jnp.float32
    )
    gate = gate_up[:, :hidden]
    activated = (gate / (1.0 + jnp.exp(-gate)) * gate_up[:, hidden:]).astype(jnp.bfloat16)
    half = jnp.dot(activated, w_out_ref[0], preferred_element_type=jnp.float32)
    weighted[pl.ds(step, 1)] = (half * row_gate).astype(jnp.bfloat16)[None]

    @pl.when(step == steps - 1)
    def _():
        for begin in range(0, count, CHUNK):
            part = pl.ds(begin, CHUNK)
            hits = jnp.concatenate(
                [
                    chosen(base_ref[0] + j, part).astype(jnp.float32).astype(jnp.bfloat16)
                    for j in range(weighted.shape[0])
                ],
                axis=0,
            )
            out_ref[part, :] = lax.dot_general(
                hits, weighted[...].reshape(-1, weighted.shape[2]),
                (((0,), (0,)), ((), ())), preferred_element_type=jnp.float32,
            ).astype(jnp.bfloat16)


def run_experts(base, x, router_t, routes_t, w_in, w_out, devices):
    count, width = x.shape
    halves_here, hidden, _ = w_out.shape
    rows = CAPE * devices
    whole = functools.partial(pl.BlockSpec, pipeline_mode=pl.Buffered(1))
    return pl.pallas_call(
        experts_kernel,
        grid=(halves_here,),
        in_specs=[
            pl.BlockSpec(memory_space=pltpu.SMEM),
            whole((count, width), lambda j: (0, 0)),
            whole(router_t.shape, lambda j: (0, 0)),
            whole(routes_t.shape, lambda j: (0, 0)),
            pl.BlockSpec((1,) + w_in.shape[1:], lambda j: (j, 0, 0)),
            pl.BlockSpec((1,) + w_out.shape[1:], lambda j: (j, 0, 0)),
        ],
        out_specs=whole((count, width), lambda j: (0, 0)),
        out_shape=jax.ShapeDtypeStruct((count, width), jnp.bfloat16),
        scratch_shapes=[
            pltpu.VMEM((EXPERTS, count), jnp.float32),
            pltpu.VMEM((EXPERTS, count), jnp.float32),
            pltpu.VMEM((halves_here, rows, width), jnp.bfloat16),
        ],
        compiler_params=pltpu.CompilerParams(vmem_limit_bytes=60 << 20),
        cost_estimate=pl.CostEstimate(
            flops=20 * 10**9, bytes_accessed=45 * 10**6, transcendentals=10**6
        ),
    )(base, x, router_t, routes_t, w_in, w_out)


def per_device(tokens, routes, router, w_in, w_out, cache_prefill, page_slot):
    devices = lax.axis_size(AXES)
    me = lax.axis_index(AXES)
    pages_here, page_width = cache_prefill.shape
    page_cap = pages_here // devices + 1
    tok_count, top_count = routes.shape
    halves_here = w_in.shape[0]

    target = page_slot // pages_here
    same = target[:, None] == target[None, :]
    earlier = jnp.arange(pages_here)[None, :] < jnp.arange(pages_here)[:, None]
    placed = target * page_cap + jnp.sum((same & earlier).astype(jnp.int32), axis=1)
    send_pick = (jnp.arange(devices * page_cap)[:, None] == placed[None, :]).astype(jnp.bfloat16)
    outgoing = jnp.dot(send_pick, cache_prefill, preferred_element_type=jnp.float32).astype(
        jnp.bfloat16
    )
    arrived = lax.all_to_all(outgoing, AXES, split_axis=0, concat_axis=0, tiled=True)

    numbers = jnp.concatenate([routes.reshape(-1), page_slot])
    numbers = lax.all_gather(numbers[None], AXES, axis=0, tiled=True)
    x = lax.all_gather(tokens, AXES, axis=0, tiled=True)
    all_routes = numbers[:, : tok_count * top_count].reshape(devices * tok_count, top_count)
    base = jnp.reshape((me * halves_here) % EXPERTS, (1,)).astype(jnp.int32)
    partial = run_experts(base, x, router.T, all_routes.T, w_in, w_out, devices)
    moe_out = lax.psum_scatter(partial, AXES, scatter_dimension=0, tiled=True)

    slots = numbers[:, tok_count * top_count :]
    mine = slots // pages_here == me
    order = jnp.sum((mine[:, None, :] & earlier[None]).astype(jnp.int32), axis=2)
    taken = mine[:, None, :] & (order[:, None, :] == jnp.arange(page_cap)[None, :, None])
    landing = jnp.sum(jnp.where(taken, slots[:, None, :] % pages_here + 1, 0), axis=2) - 1
    land_pick = (jnp.arange(pages_here)[:, None] == landing.reshape(1, -1)).astype(jnp.bfloat16)
    cache_decode = jnp.dot(land_pick, arrived, preferred_element_type=jnp.float32).astype(
        jnp.bfloat16
    )
    return moe_out, cache_decode


def solution(mesh):
    in_specs = (
        P(AXES, None),
        P(AXES, None),
        P(),
        P(AXES, None, None),
        P(AXES, None, None),
        P(AXES, None),
        P(AXES),
    )
    out_specs = (P(AXES, None), P(AXES, None))
    return jax.shard_map(
        per_device, mesh=mesh, in_specs=in_specs, out_specs=out_specs, check_vma=False
    )
```

```python
import functools

import jax
import jax.numpy as jnp
from jax import lax
from jax.experimental import pallas as pl
from jax.experimental.pallas import tpu as pltpu
from jax.sharding import PartitionSpec as P

EXPERTS = 64
CAPE = 6
AXES = ("row", "col")
ROUTE_SCALE = 2.446
CHUNK = 512
TOP = 6
MESH = pl.DeviceIdType.MESH
FUSED_TOKENS = 1024


def experts_kernel(base_ref, x_ref, router_ref, routes_ref, w_in_ref, w_out_ref, out_ref,
                   gates, ranks, weighted):
    step = pl.program_id(0)
    steps = pl.num_programs(0)
    count = x_ref.shape[0]
    rows = weighted.shape[1]
    hidden = w_out_ref.shape[1]

    @pl.when(step == 0)
    def _():
        expert_row = lax.broadcasted_iota(jnp.int32, (EXPERTS, CHUNK), 0)
        earlier = (
            lax.broadcasted_iota(jnp.int32, (CHUNK, CHUNK), 0)
            < lax.broadcasted_iota(jnp.int32, (CHUNK, CHUNK), 1)
        ).astype(jnp.float32).astype(jnp.bfloat16)
        offset = jnp.zeros((EXPERTS, 1), jnp.float32)
        for begin in range(0, count, CHUNK):
            part = slice(begin, begin + CHUNK)
            logits = lax.dot_general(
                router_ref[...], x_ref[part, :], (((1,), (1,)), ((), ())),
                preferred_element_type=jnp.float32,
            )
            scores = 1.0 / (1.0 + jnp.exp(-logits))
            named = jnp.zeros((EXPERTS, CHUNK), jnp.float32)
            for k in range(routes_ref.shape[0]):
                named = jnp.where(routes_ref[k : k + 1, part] == expert_row, 1.0, named)
            picked = scores * named
            gates[:, part] = ROUTE_SCALE * picked / jnp.sum(picked, axis=0, keepdims=True)
            before = offset + jnp.dot(
                named.astype(jnp.bfloat16), earlier, preferred_element_type=jnp.float32
            )
            ranks[:, part] = jnp.where(named > 0.0, before, -1.0)
            offset = offset + jnp.sum(named, axis=1, keepdims=True)

    expert = base_ref[0] + step

    def chosen(which, part):
        slots = lax.broadcasted_iota(jnp.int32, (rows, part.size), 0).astype(jnp.float32)
        return ranks[pl.ds(which, 1), part] == slots

    picked_rows = jnp.zeros((rows, x_ref.shape[1]), jnp.float32)
    row_gate = jnp.zeros((rows, 1), jnp.float32)
    for begin in range(0, count, CHUNK):
        part = pl.ds(begin, CHUNK)
        hit = chosen(expert, part)
        picked_rows += jnp.dot(
            hit.astype(jnp.float32).astype(jnp.bfloat16), x_ref[part, :],
            preferred_element_type=jnp.float32,
        )
        row_gate += jnp.sum(
            jnp.where(hit, gates[pl.ds(expert, 1), part], 0.0), axis=1, keepdims=True
        )
    gate_up = jnp.dot(
        picked_rows.astype(jnp.bfloat16), w_in_ref[0], preferred_element_type=jnp.float32
    )
    gate = gate_up[:, :hidden]
    activated = (gate / (1.0 + jnp.exp(-gate)) * gate_up[:, hidden:]).astype(jnp.bfloat16)
    half = jnp.dot(activated, w_out_ref[0], preferred_element_type=jnp.float32)
    weighted[pl.ds(step, 1)] = (half * row_gate).astype(jnp.bfloat16)[None]

    @pl.when(step == steps - 1)
    def _():
        for begin in range(0, count, CHUNK):
            part = pl.ds(begin, CHUNK)
            hits = jnp.concatenate(
                [
                    chosen(base_ref[0] + j, part).astype(jnp.float32).astype(jnp.bfloat16)
                    for j in range(weighted.shape[0])
                ],
                axis=0,
            )
            out_ref[part, :] = lax.dot_general(
                hits, weighted[...].reshape(-1, weighted.shape[2]),
                (((0,), (0,)), ((), ())), preferred_element_type=jnp.float32,
            ).astype(jnp.bfloat16)


def run_experts(base, x, router_t, routes_t, w_in, w_out, devices):
    count, width = x.shape
    halves_here, hidden, _ = w_out.shape
    rows = CAPE * devices
    whole = functools.partial(pl.BlockSpec, pipeline_mode=pl.Buffered(1))
    return pl.pallas_call(
        experts_kernel,
        grid=(halves_here,),
        in_specs=[
            pl.BlockSpec(memory_space=pltpu.SMEM),
            whole((count, width), lambda j: (0, 0)),
            whole(router_t.shape, lambda j: (0, 0)),
            whole(routes_t.shape, lambda j: (0, 0)),
            pl.BlockSpec((1,) + w_in.shape[1:], lambda j: (j, 0, 0)),
            pl.BlockSpec((1,) + w_out.shape[1:], lambda j: (j, 0, 0)),
        ],
        out_specs=whole((count, width), lambda j: (0, 0)),
        out_shape=jax.ShapeDtypeStruct((count, width), jnp.bfloat16),
        scratch_shapes=[
            pltpu.VMEM((EXPERTS, count), jnp.float32),
            pltpu.VMEM((EXPERTS, count), jnp.float32),
            pltpu.VMEM((halves_here, rows, width), jnp.bfloat16),
        ],
        compiler_params=pltpu.CompilerParams(vmem_limit_bytes=60 << 20),
        cost_estimate=pl.CostEstimate(
            flops=20 * 10**9, bytes_accessed=45 * 10**6, transcendentals=10**6
        ),
    )(base, x, router_t, routes_t, w_in, w_out)


def bits_of(number, count):
    return [(number // 2 ** (count - 1 - b)) % 2 for b in range(count)]


def fused_kernel(n_row, n_col, tokens_ref, router_ref, numbers_ref, pages_ref, w_in_hbm, w_out_hbm,
                 out_ref, arrived_ref, all_numbers_ref,
                 x, part, gates, ranks, weighted, w_in_buf, w_out_buf, *rest):
    devices = n_row * n_col
    dims = devices.bit_length() - 1
    row_bits = n_row.bit_length() - 1
    sends, receives = rest[:dims], rest[dims : 2 * dims]
    (w_sem, own_sem, page_send, page_recv, gather_send, gather_recv,
     sum_send, sum_recv) = rest[2 * dims :]
    row, col = lax.axis_index("row"), lax.axis_index("col")
    me = row * n_col + col
    mine = bits_of(me, dims)
    tok_count, width = tokens_ref.shape
    halves_here, hidden, _ = w_out_hbm.shape
    rows = weighted.shape[1]
    split = width // 2
    columns = [pl.ds(0, split), pl.ds(split, split)]
    inner = list(range(row_bits, dims - 1))
    orders = [
        list(range(row_bits)) + inner + [dims - 1],
        list(range(row_bits)) + inner[::-1] + [dims - 1],
    ]

    def place(number):
        return (number // n_col, number % n_col)

    def partner(b):
        return place(me + (1 - 2 * mine[b]) * 2 ** (dims - 1 - b))

    def weights(j, slot):
        return (
            pltpu.make_async_copy(w_in_hbm.at[j], w_in_buf.at[slot], w_sem.at[slot, 0]),
            pltpu.make_async_copy(w_out_hbm.at[j], w_out_buf.at[slot], w_sem.at[slot, 1]),
        )

    slots = w_in_buf.shape[0]
    for j in range(min(slots, halves_here)):
        for copy in weights(j, j):
            copy.start()
    own = pltpu.make_async_copy(pages_ref.at[me], arrived_ref.at[me], own_sem)
    own.start()

    barrier = pltpu.get_barrier_semaphore()

    @pl.loop(1, devices)
    def _(o):
        pl.semaphore_signal(barrier, inc=1, device_id=place((me + o) % devices), device_id_type=MESH)

    x[tuple(mine)] = tokens_ref[...]
    all_numbers_ref[tuple(mine)] = numbers_ref[...]
    pl.semaphore_wait(barrier, devices - 1)

    def page(o):
        to = (me + o) % devices
        return pltpu.make_async_remote_copy(
            src_ref=pages_ref.at[to], dst_ref=arrived_ref.at[me],
            send_sem=page_send.at[o], recv_sem=page_recv.at[o],
            device_id=place(to), device_id_type=MESH,
        )

    for s in range(dims):
        copies = []
        for h in range(3):
            order = orders[h % 2]
            done, b = order[:s], order[s]
            index = tuple(slice(None) if d in done else mine[d] for d in range(dims))
            if h < 2:
                ref = x.at[index + (slice(None), columns[h])]
            else:
                ref = all_numbers_ref.at[index]
            copies.append(
                pltpu.make_async_remote_copy(
                    src_ref=ref, dst_ref=ref,
                    send_sem=gather_send.at[s, h], recv_sem=gather_recv.at[s, h],
                    device_id=partner(b), device_id_type=MESH,
                )
            )
        for copy in copies:
            copy.start()
        for copy in copies:
            copy.wait()
        if s == row_bits - 1:

            @pl.loop(1, devices)
            def _(o):
                page(o).start()

    chunk = devices // 2 * tok_count
    group = 128 // tok_count

    def tokens_of(q):
        return x[q].reshape(chunk, width)

    expert_row = lax.broadcasted_iota(jnp.int32, (EXPERTS, chunk), 0)
    earlier = (
        lax.broadcasted_iota(jnp.int32, (chunk, chunk), 0)
        < lax.broadcasted_iota(jnp.int32, (chunk, chunk), 1)
    ).astype(jnp.float32).astype(jnp.bfloat16)
    offset = jnp.zeros((EXPERTS, 1), jnp.float32)
    for q in range(2):
        part_q = slice(q * chunk, (q + 1) * chunk)
        numbers = all_numbers_ref[q].reshape(-1, group, 8, 128)
        numbers = [
            functools.reduce(lambda a, b: a + b, [numbers[i, g] for g in range(group)])
            for i in range(numbers.shape[0])
        ]
        routes = jnp.concatenate(numbers, axis=1)
        logits = lax.dot_general(
            router_ref[...], tokens_of(q), (((1,), (1,)), ((), ())),
            preferred_element_type=jnp.float32,
        )
        scores = 1.0 / (1.0 + jnp.exp(-logits))
        named = jnp.zeros((EXPERTS, chunk), jnp.float32)
        for k in range(TOP):
            named = jnp.where(routes[k : k + 1, :] == expert_row, 1.0, named)
        picked = scores * named
        gates[:, part_q] = ROUTE_SCALE * picked / jnp.sum(picked, axis=0, keepdims=True)
        before = offset + jnp.dot(
            named.astype(jnp.bfloat16), earlier, preferred_element_type=jnp.float32
        )
        ranks[:, part_q] = jnp.where(named > 0.0, before, -1.0)
        offset = offset + jnp.sum(named, axis=1, keepdims=True)

    base = (me * halves_here) % EXPERTS

    def chosen(which, q):
        numbering = lax.broadcasted_iota(jnp.int32, (rows, chunk), 0).astype(jnp.float32)
        return ranks[pl.ds(which, 1), q * chunk : (q + 1) * chunk] == numbering

    @pl.loop(0, halves_here)
    def _(j):
        slot = j % slots
        expert = base + j
        picked_rows = jnp.zeros((rows, width), jnp.float32)
        row_gate = jnp.zeros((rows, 1), jnp.float32)
        for q in range(2):
            hit = chosen(expert, q)
            picked_rows += jnp.dot(
                hit.astype(jnp.float32).astype(jnp.bfloat16), tokens_of(q),
                preferred_element_type=jnp.float32,
            )
            row_gate += jnp.sum(
                jnp.where(hit, gates[pl.ds(expert, 1), q * chunk : (q + 1) * chunk], 0.0),
                axis=1, keepdims=True,
            )
        w_first, w_second = weights(j, slot)
        w_first.wait()
        gate_up = jnp.dot(
            picked_rows.astype(jnp.bfloat16), w_in_buf[slot], preferred_element_type=jnp.float32
        )
        gate = gate_up[:, :hidden]
        activated = (gate / (1.0 + jnp.exp(-gate)) * gate_up[:, hidden:]).astype(jnp.bfloat16)
        w_second.wait()
        half = jnp.dot(activated, w_out_buf[slot], preferred_element_type=jnp.float32)
        weighted[pl.ds(j, 1)] = (half * row_gate).astype(jnp.bfloat16)[None]

        @pl.when(j + slots < halves_here)
        def _():
            for copy in weights(j + slots, slot):
                copy.start()

    for q in range(2):
        hits = jnp.concatenate(
            [
                chosen(base + j, q).astype(jnp.float32).astype(jnp.bfloat16)
                for j in range(halves_here)
            ],
            axis=0,
        )
        part[pl.ds(q * (devices // 2), devices // 2)] = lax.dot_general(
            hits, weighted[...].reshape(halves_here * rows, width),
            (((0,), (0,)), ((), ())), preferred_element_type=jnp.float32,
        ).reshape(devices // 2, tok_count, width)

    def blocks(order, s, flip):
        fixed = {b: mine[b] for b in order[:s]}
        fixed[order[s]] = 1 - mine[order[s]] if flip else mine[order[s]]
        free = sorted(order[s + 1 :])
        for i in range(2 ** len(free)):
            bits = dict(fixed)
            for place_of, d in enumerate(free):
                bits[d] = (i >> (len(free) - 1 - place_of)) & 1
            yield i, sum(bits[d] * 2 ** (dims - 1 - d) for d in range(dims))

    for s in range(dims):
        copies = []
        for h in range(2):
            order = orders[h][::-1]
            for i, block in blocks(order, s, True):
                sends[s][i, :, columns[h]] = part[block, :, columns[h]].astype(jnp.bfloat16)
            copy = pltpu.make_async_remote_copy(
                src_ref=sends[s].at[:, :, columns[h]], dst_ref=receives[s].at[:, :, columns[h]],
                send_sem=sum_send.at[s, h], recv_sem=sum_recv.at[s, h],
                device_id=partner(order[s]), device_id_type=MESH,
            )
            copy.start()
            copies.append(copy)
        for h in range(2):
            copies[h].wait()
            for i, block in blocks(orders[h][::-1], s, False):
                part[block, :, columns[h]] += receives[s][i, :, columns[h]].astype(jnp.float32)
    out_ref[...] = part[me].astype(jnp.bfloat16)

    own.wait()

    @pl.loop(1, devices)
    def _(o):
        page(o).wait()


def run_fused(n_row, n_col, tokens, router_t, numbers, pages, w_in, w_out):
    devices = n_row * n_col
    dims = devices.bit_length() - 1
    tok_count, width = tokens.shape
    halves_here, hidden, _ = w_out.shape
    count = devices * tok_count
    rows = CAPE * devices
    cube = (2,) * dims
    slots = min(2, halves_here)
    vmem = pl.BlockSpec(memory_space=pltpu.VMEM)
    anywhere = pl.BlockSpec(memory_space=pl.ANY)
    parts = [pltpu.VMEM((2 ** (dims - 1 - s), tok_count, width), jnp.bfloat16) for s in range(dims)]
    return pl.pallas_call(
        functools.partial(fused_kernel, n_row, n_col),
        in_specs=[vmem, vmem, vmem, anywhere, anywhere, anywhere],
        out_specs=[vmem, anywhere, vmem],
        out_shape=[
            jax.ShapeDtypeStruct((tok_count, width), jnp.bfloat16),
            jax.ShapeDtypeStruct(pages.shape, jnp.bfloat16),
            jax.ShapeDtypeStruct(cube + numbers.shape, jnp.int32),
        ],
        scratch_shapes=[
            pltpu.VMEM(cube + (tok_count, width), jnp.bfloat16),
            pltpu.VMEM((devices, tok_count, width), jnp.float32),
            pltpu.VMEM((EXPERTS, count), jnp.float32),
            pltpu.VMEM((EXPERTS, count), jnp.float32),
            pltpu.VMEM((halves_here, rows, width), jnp.bfloat16),
            pltpu.VMEM((slots,) + w_in.shape[1:], jnp.bfloat16),
            pltpu.VMEM((slots,) + w_out.shape[1:], jnp.bfloat16),
            *parts,
            *parts,
            pltpu.SemaphoreType.DMA((slots, 2)),
            pltpu.SemaphoreType.DMA(()),
            pltpu.SemaphoreType.DMA((devices,)),
            pltpu.SemaphoreType.DMA((devices,)),
            pltpu.SemaphoreType.DMA((dims, 3)),
            pltpu.SemaphoreType.DMA((dims, 3)),
            pltpu.SemaphoreType.DMA((dims, 2)),
            pltpu.SemaphoreType.DMA((dims, 2)),
        ],
        compiler_params=pltpu.CompilerParams(
            collective_id=0, has_side_effects=True, vmem_limit_bytes=60 << 20
        ),
        cost_estimate=pl.CostEstimate(
            flops=20 * 10**9, bytes_accessed=45 * 10**6, transcendentals=10**6
        ),
    )(tokens, router_t, numbers, pages, w_in, w_out)


def per_device(tokens, routes, router, w_in, w_out, cache_prefill, page_slot):
    devices = lax.axis_size(AXES)
    me = lax.axis_index(AXES)
    pages_here, page_width = cache_prefill.shape
    page_cap = pages_here // devices + 1
    tok_count, top_count = routes.shape
    halves_here = w_in.shape[0]

    target = page_slot // pages_here
    same = target[:, None] == target[None, :]
    earlier = jnp.arange(pages_here)[None, :] < jnp.arange(pages_here)[:, None]
    placed = target * page_cap + jnp.sum((same & earlier).astype(jnp.int32), axis=1)
    send_pick = (jnp.arange(devices * page_cap)[:, None] == placed[None, :]).astype(jnp.bfloat16)
    outgoing = jnp.dot(send_pick, cache_prefill, preferred_element_type=jnp.float32).astype(
        jnp.bfloat16
    )
    if devices * tok_count <= FUSED_TOKENS and tok_count * 4 <= 128:
        pad = -(page_cap * page_width) % (16 * 128)
        pages = outgoing.reshape(devices, page_cap * page_width)
        pages = jnp.pad(pages, ((0, 0), (0, pad))).reshape(devices, -1, 128)
        lane = jnp.arange(128) // tok_count
        spread = jnp.tile(routes.T, (1, 128 // tok_count))
        spread = jnp.where(lane[None, :] == me % (128 // tok_count), spread, 0)
        block = jnp.concatenate(
            [
                spread,
                jnp.pad(page_slot, (0, 128 - pages_here))[None],
                jnp.zeros((7 - top_count, 128), jnp.int32),
            ],
            axis=0,
        )
        moe_out, arrived, numbers = run_fused(
            lax.axis_size("row"), lax.axis_size("col"), tokens, router.T, block, pages, w_in, w_out
        )
        arrived = arrived.reshape(devices, -1)[:, : page_cap * page_width]
        arrived = arrived.reshape(devices * page_cap, page_width)
        slots = numbers.reshape(devices, 8, 128)[:, top_count, :pages_here]
    else:
        arrived = lax.all_to_all(outgoing, AXES, split_axis=0, concat_axis=0, tiled=True)

        numbers = jnp.concatenate([routes.reshape(-1), page_slot])
        numbers = lax.all_gather(numbers[None], AXES, axis=0, tiled=True)
        x = lax.all_gather(tokens, AXES, axis=0, tiled=True)
        all_routes = numbers[:, : tok_count * top_count].reshape(devices * tok_count, top_count)
        base = jnp.reshape((me * halves_here) % EXPERTS, (1,)).astype(jnp.int32)
        partial = run_experts(base, x, router.T, all_routes.T, w_in, w_out, devices)
        moe_out = lax.psum_scatter(partial, AXES, scatter_dimension=0, tiled=True)
        slots = numbers[:, tok_count * top_count :]

    mine = slots // pages_here == me
    order = jnp.sum((mine[:, None, :] & earlier[None]).astype(jnp.int32), axis=2)
    taken = mine[:, None, :] & (order[:, None, :] == jnp.arange(page_cap)[None, :, None])
    landing = jnp.sum(jnp.where(taken, slots[:, None, :] % pages_here + 1, 0), axis=2) - 1
    land_pick = (jnp.arange(pages_here)[:, None] == landing.reshape(1, -1)).astype(jnp.bfloat16)
    cache_decode = jnp.dot(land_pick, arrived, preferred_element_type=jnp.float32).astype(
        jnp.bfloat16
    )
    return moe_out, cache_decode


def solution(mesh):
    in_specs = (
        P(AXES, None),
        P(AXES, None),
        P(),
        P(AXES, None, None),
        P(AXES, None, None),
        P(AXES, None),
        P(AXES),
    )
    out_specs = (P(AXES, None), P(AXES, None))
    return jax.shard_map(
        per_device, mesh=mesh, in_specs=in_specs, out_specs=out_specs, check_vma=False
    )
```

```python
import functools

import jax
import jax.numpy as jnp
from jax import lax
from jax.experimental import pallas as pl
from jax.experimental.pallas import tpu as pltpu
from jax.sharding import PartitionSpec as P

EXPERTS = 64
CAPE = 6
AXES = ("row", "col")
ROUTE_SCALE = 2.446
CHUNK = 512
TOP = 6
MESH = pl.DeviceIdType.MESH
FUSED_TOKENS = 1024


def experts_kernel(base_ref, x_ref, router_ref, routes_ref, w_in_ref, w_out_ref, out_ref,
                   gates, ranks, weighted):
    step = pl.program_id(0)
    steps = pl.num_programs(0)
    count = x_ref.shape[0]
    rows = weighted.shape[1]
    hidden = w_out_ref.shape[1]

    @pl.when(step == 0)
    def _():
        expert_row = lax.broadcasted_iota(jnp.int32, (EXPERTS, CHUNK), 0)
        earlier = (
            lax.broadcasted_iota(jnp.int32, (CHUNK, CHUNK), 0)
            < lax.broadcasted_iota(jnp.int32, (CHUNK, CHUNK), 1)
        ).astype(jnp.float32).astype(jnp.bfloat16)
        offset = jnp.zeros((EXPERTS, 1), jnp.float32)
        for begin in range(0, count, CHUNK):
            part = slice(begin, begin + CHUNK)
            logits = lax.dot_general(
                router_ref[...], x_ref[part, :], (((1,), (1,)), ((), ())),
                preferred_element_type=jnp.float32,
            )
            scores = 1.0 / (1.0 + jnp.exp(-logits))
            named = jnp.zeros((EXPERTS, CHUNK), jnp.float32)
            for k in range(routes_ref.shape[0]):
                named = jnp.where(routes_ref[k : k + 1, part] == expert_row, 1.0, named)
            picked = scores * named
            gates[:, part] = ROUTE_SCALE * picked / jnp.sum(picked, axis=0, keepdims=True)
            before = offset + jnp.dot(
                named.astype(jnp.bfloat16), earlier, preferred_element_type=jnp.float32
            )
            ranks[:, part] = jnp.where(named > 0.0, before, -1.0)
            offset = offset + jnp.sum(named, axis=1, keepdims=True)

    expert = base_ref[0] + step

    def chosen(which, part):
        slots = lax.broadcasted_iota(jnp.int32, (rows, part.size), 0).astype(jnp.float32)
        return ranks[pl.ds(which, 1), part] == slots

    picked_rows = jnp.zeros((rows, x_ref.shape[1]), jnp.float32)
    row_gate = jnp.zeros((rows, 1), jnp.float32)
    for begin in range(0, count, CHUNK):
        part = pl.ds(begin, CHUNK)
        hit = chosen(expert, part)
        picked_rows += jnp.dot(
            hit.astype(jnp.float32).astype(jnp.bfloat16), x_ref[part, :],
            preferred_element_type=jnp.float32,
        )
        row_gate += jnp.sum(
            jnp.where(hit, gates[pl.ds(expert, 1), part], 0.0), axis=1, keepdims=True
        )
    gate_up = jnp.dot(
        picked_rows.astype(jnp.bfloat16), w_in_ref[0], preferred_element_type=jnp.float32
    )
    gate = gate_up[:, :hidden]
    activated = (gate / (1.0 + jnp.exp(-gate)) * gate_up[:, hidden:]).astype(jnp.bfloat16)
    half = jnp.dot(activated, w_out_ref[0], preferred_element_type=jnp.float32)
    weighted[pl.ds(step, 1)] = (half * row_gate).astype(jnp.bfloat16)[None]

    @pl.when(step == steps - 1)
    def _():
        for begin in range(0, count, CHUNK):
            part = pl.ds(begin, CHUNK)
            hits = jnp.concatenate(
                [
                    chosen(base_ref[0] + j, part).astype(jnp.float32).astype(jnp.bfloat16)
                    for j in range(weighted.shape[0])
                ],
                axis=0,
            )
            out_ref[part, :] = lax.dot_general(
                hits, weighted[...].reshape(-1, weighted.shape[2]),
                (((0,), (0,)), ((), ())), preferred_element_type=jnp.float32,
            ).astype(jnp.bfloat16)


def run_experts(base, x, router_t, routes_t, w_in, w_out, devices):
    count, width = x.shape
    halves_here, hidden, _ = w_out.shape
    rows = CAPE * devices
    whole = functools.partial(pl.BlockSpec, pipeline_mode=pl.Buffered(1))
    return pl.pallas_call(
        experts_kernel,
        grid=(halves_here,),
        in_specs=[
            pl.BlockSpec(memory_space=pltpu.SMEM),
            whole((count, width), lambda j: (0, 0)),
            whole(router_t.shape, lambda j: (0, 0)),
            whole(routes_t.shape, lambda j: (0, 0)),
            pl.BlockSpec((1,) + w_in.shape[1:], lambda j: (j, 0, 0)),
            pl.BlockSpec((1,) + w_out.shape[1:], lambda j: (j, 0, 0)),
        ],
        out_specs=whole((count, width), lambda j: (0, 0)),
        out_shape=jax.ShapeDtypeStruct((count, width), jnp.bfloat16),
        scratch_shapes=[
            pltpu.VMEM((EXPERTS, count), jnp.float32),
            pltpu.VMEM((EXPERTS, count), jnp.float32),
            pltpu.VMEM((halves_here, rows, width), jnp.bfloat16),
        ],
        compiler_params=pltpu.CompilerParams(vmem_limit_bytes=60 << 20),
        cost_estimate=pl.CostEstimate(
            flops=20 * 10**9, bytes_accessed=45 * 10**6, transcendentals=10**6
        ),
    )(base, x, router_t, routes_t, w_in, w_out)


def bits_of(number, count):
    return [(number // 2 ** (count - 1 - b)) % 2 for b in range(count)]


def fused_kernel(n_row, n_col, tokens_ref, router_ref, numbers_ref, pages_ref, w_in_hbm, w_out_hbm,
                 out_ref, arrived_ref, all_numbers_ref,
                 x, part, gates, ranks, weighted, activated, row_gates, w_in_buf, w_out_buf, *rest):
    devices = n_row * n_col
    dims = devices.bit_length() - 1
    row_bits = n_row.bit_length() - 1
    sends, receives = rest[:dims], rest[dims : 2 * dims]
    (w_sem, v_sem, own_sem, page_send, page_recv, gather_send, gather_recv,
     sum_send, sum_recv) = rest[2 * dims :]
    row, col = lax.axis_index("row"), lax.axis_index("col")
    me = row * n_col + col
    mine = bits_of(me, dims)
    tok_count, width = tokens_ref.shape
    halves_here, hidden, _ = w_out_hbm.shape
    rows = weighted.shape[1]
    split = width // 4
    columns = [pl.ds(c * split, split) for c in range(4)]
    inner = list(range(row_bits, dims - 1))
    orders = [
        list(range(row_bits)) + inner + [dims - 1],
        list(range(row_bits)) + inner[::-1] + [dims - 1],
    ]

    def place(number):
        return (number // n_col, number % n_col)

    def partner(b):
        return place(me + (1 - 2 * mine[b]) * 2 ** (dims - 1 - b))

    slots = w_in_buf.shape[0]

    def first_weights(j):
        slot = j % slots
        return pltpu.make_async_copy(w_in_hbm.at[j], w_in_buf.at[slot], w_sem.at[slot])

    def second_weights(j):
        return pltpu.make_async_copy(w_out_hbm.at[j], w_out_buf.at[j], v_sem.at[j])

    for j in range(slots):
        first_weights(j).start()
    for j in range(halves_here):
        second_weights(j).start()
    own = pltpu.make_async_copy(pages_ref.at[me], arrived_ref.at[me], own_sem)
    own.start()

    barrier = pltpu.get_barrier_semaphore()

    @pl.loop(1, devices)
    def _(o):
        pl.semaphore_signal(barrier, inc=1, device_id=place((me + o) % devices), device_id_type=MESH)

    x[tuple(mine)] = tokens_ref[...]
    all_numbers_ref[tuple(mine)] = numbers_ref[...]
    pl.semaphore_wait(barrier, devices - 1)

    def page(o):
        to = (me + o) % devices
        return pltpu.make_async_remote_copy(
            src_ref=pages_ref.at[to], dst_ref=arrived_ref.at[me],
            send_sem=page_send.at[o], recv_sem=page_recv.at[o],
            device_id=place(to), device_id_type=MESH,
        )

    def gather(g, s):
        copies = []
        for h in range(3 - g):
            order = orders[h % 2]
            done, b = order[:s], order[s]
            index = tuple(slice(None) if d in done else mine[d] for d in range(dims))
            if h < 2:
                ref = x.at[index + (slice(None), columns[2 * g + h])]
            else:
                ref = all_numbers_ref.at[index]
            copies.append(
                pltpu.make_async_remote_copy(
                    src_ref=ref, dst_ref=ref,
                    send_sem=gather_send.at[s, 2 * h + g], recv_sem=gather_recv.at[s, 2 * h + g],
                    device_id=partner(b), device_id_type=MESH,
                )
            )
        return copies

    for tick in range(dims + 1):
        for g in range(2):
            s = tick - g
            if 0 < s <= dims:
                for copy in gather(g, s - 1):
                    copy.wait()
            if 0 <= s < dims:
                for copy in gather(g, s):
                    copy.start()

    @pl.loop(1, devices)
    def _(o):
        page(o).start()

    for copy in gather(1, dims - 1):
        copy.wait()

    chunk = devices // 2 * tok_count
    group = 128 // tok_count

    def tokens_of(q):
        return x[q].reshape(chunk, width)

    expert_row = lax.broadcasted_iota(jnp.int32, (EXPERTS, chunk), 0)
    earlier = (
        lax.broadcasted_iota(jnp.int32, (chunk, chunk), 0)
        < lax.broadcasted_iota(jnp.int32, (chunk, chunk), 1)
    ).astype(jnp.float32).astype(jnp.bfloat16)
    offset = jnp.zeros((EXPERTS, 1), jnp.float32)
    for q in range(2):
        part_q = slice(q * chunk, (q + 1) * chunk)
        numbers = all_numbers_ref[q].reshape(-1, group, 8, 128)
        numbers = [
            functools.reduce(lambda a, b: a + b, [numbers[i, g] for g in range(group)])
            for i in range(numbers.shape[0])
        ]
        routes = jnp.concatenate(numbers, axis=1)
        logits = lax.dot_general(
            router_ref[...], tokens_of(q), (((1,), (1,)), ((), ())),
            preferred_element_type=jnp.float32,
        )
        scores = 1.0 / (1.0 + jnp.exp(-logits))
        named = jnp.zeros((EXPERTS, chunk), jnp.float32)
        for k in range(TOP):
            named = jnp.where(routes[k : k + 1, :] == expert_row, 1.0, named)
        picked = scores * named
        gates[:, part_q] = ROUTE_SCALE * picked / jnp.sum(picked, axis=0, keepdims=True)
        before = offset + jnp.dot(
            named.astype(jnp.bfloat16), earlier, preferred_element_type=jnp.float32
        )
        ranks[:, part_q] = jnp.where(named > 0.0, before, -1.0)
        offset = offset + jnp.sum(named, axis=1, keepdims=True)

    base = (me * halves_here) % EXPERTS

    def chosen(which, q):
        numbering = lax.broadcasted_iota(jnp.int32, (rows, chunk), 0).astype(jnp.float32)
        return ranks[pl.ds(which, 1), q * chunk : (q + 1) * chunk] == numbering

    @pl.loop(0, halves_here)
    def _(j):
        expert = base + j
        picked_rows = jnp.zeros((rows, width), jnp.float32)
        row_gate = jnp.zeros((rows, 1), jnp.float32)
        for q in range(2):
            hit = chosen(expert, q)
            picked_rows += jnp.dot(
                hit.astype(jnp.float32).astype(jnp.bfloat16), tokens_of(q),
                preferred_element_type=jnp.float32,
            )
            row_gate += jnp.sum(
                jnp.where(hit, gates[pl.ds(expert, 1), q * chunk : (q + 1) * chunk], 0.0),
                axis=1, keepdims=True,
            )
        row_gates[pl.ds(j, 1)] = row_gate[None]
        first_weights(j).wait()
        gate_up = jnp.dot(
            picked_rows.astype(jnp.bfloat16), w_in_buf[j % slots],
            preferred_element_type=jnp.float32,
        )
        gate = gate_up[:, :hidden]
        activated[pl.ds(j, 1)] = (
            gate / (1.0 + jnp.exp(-gate)) * gate_up[:, hidden:]
        ).astype(jnp.bfloat16)[None]

        @pl.when(j + slots < halves_here)
        def _():
            first_weights(j + slots).start()

    for j in range(halves_here):
        second_weights(j).wait()

    def sum_experts(g):
        begin, size = 2 * g * split, 2 * split
        for j in range(halves_here):
            half = jnp.dot(
                activated[j], w_out_buf[j, :, begin : begin + size],
                preferred_element_type=jnp.float32,
            )
            weighted[j, :, begin : begin + size] = (half * row_gates[j]).astype(jnp.bfloat16)
        for q in range(2):
            hits = jnp.concatenate(
                [
                    chosen(base + j, q).astype(jnp.float32).astype(jnp.bfloat16)
                    for j in range(halves_here)
                ],
                axis=0,
            )
            part[pl.ds(q * (devices // 2), devices // 2), :, pl.ds(begin, size)] = lax.dot_general(
                hits, weighted[:, :, begin : begin + size].reshape(halves_here * rows, size),
                (((0,), (0,)), ((), ())), preferred_element_type=jnp.float32,
            ).reshape(devices // 2, tok_count, size)

    def blocks(order, s, flip):
        fixed = {b: mine[b] for b in order[:s]}
        fixed[order[s]] = 1 - mine[order[s]] if flip else mine[order[s]]
        free = sorted(order[s + 1 :])
        for i in range(2 ** len(free)):
            bits = dict(fixed)
            for place_of, d in enumerate(free):
                bits[d] = (i >> (len(free) - 1 - place_of)) & 1
            yield i, sum(bits[d] * 2 ** (dims - 1 - d) for d in range(dims))

    def sum_copy(g, s, h):
        cols = columns[2 * g + h]
        return pltpu.make_async_remote_copy(
            src_ref=sends[s].at[:, :, cols], dst_ref=receives[s].at[:, :, cols],
            send_sem=sum_send.at[s, 2 * h + g], recv_sem=sum_recv.at[s, 2 * h + g],
            device_id=partner(orders[h][dims - 1 - s]), device_id_type=MESH,
        )

    def sum_start(g, s):
        for h in range(2):
            cols = columns[2 * g + h]
            for i, block in blocks(orders[h][::-1], s, True):
                sends[s][i, :, cols] = part[block, :, cols].astype(jnp.bfloat16)
            sum_copy(g, s, h).start()

    def sum_finish(g, s):
        for h in range(2):
            cols = columns[2 * g + h]
            sum_copy(g, s, h).wait()
            for i, block in blocks(orders[h][::-1], s, False):
                part[block, :, cols] += receives[s][i, :, cols].astype(jnp.float32)

    sum_experts(0)
    sum_start(0, 0)
    sum_experts(1)
    for tick in range(1, dims + 2):
        for g in range(2):
            s = tick - g
            if 0 < s <= dims:
                sum_finish(g, s - 1)
            if 0 <= s < dims:
                sum_start(g, s)
    out_ref[...] = part[me].astype(jnp.bfloat16)

    own.wait()

    @pl.loop(1, devices)
    def _(o):
        page(o).wait()


def run_fused(n_row, n_col, tokens, router_t, numbers, pages, w_in, w_out):
    devices = n_row * n_col
    dims = devices.bit_length() - 1
    tok_count, width = tokens.shape
    halves_here, hidden, _ = w_out.shape
    count = devices * tok_count
    rows = CAPE * devices
    cube = (2,) * dims
    slots = min(3, halves_here)
    vmem = pl.BlockSpec(memory_space=pltpu.VMEM)
    anywhere = pl.BlockSpec(memory_space=pl.ANY)
    parts = [pltpu.VMEM((2 ** (dims - 1 - s), tok_count, width), jnp.bfloat16) for s in range(dims)]
    return pl.pallas_call(
        functools.partial(fused_kernel, n_row, n_col),
        in_specs=[vmem, vmem, vmem, anywhere, anywhere, anywhere],
        out_specs=[vmem, anywhere, vmem],
        out_shape=[
            jax.ShapeDtypeStruct((tok_count, width), jnp.bfloat16),
            jax.ShapeDtypeStruct(pages.shape, jnp.bfloat16),
            jax.ShapeDtypeStruct(cube + numbers.shape, jnp.int32),
        ],
        scratch_shapes=[
            pltpu.VMEM(cube + (tok_count, width), jnp.bfloat16),
            pltpu.VMEM((devices, tok_count, width), jnp.float32),
            pltpu.VMEM((EXPERTS, count), jnp.float32),
            pltpu.VMEM((EXPERTS, count), jnp.float32),
            pltpu.VMEM((halves_here, rows, width), jnp.bfloat16),
            pltpu.VMEM((halves_here, rows, hidden), jnp.bfloat16),
            pltpu.VMEM((halves_here, rows, 1), jnp.float32),
            pltpu.VMEM((slots,) + w_in.shape[1:], jnp.bfloat16),
            pltpu.VMEM(w_out.shape, jnp.bfloat16),
            *parts,
            *parts,
            pltpu.SemaphoreType.DMA((slots,)),
            pltpu.SemaphoreType.DMA((halves_here,)),
            pltpu.SemaphoreType.DMA(()),
            pltpu.SemaphoreType.DMA((devices,)),
            pltpu.SemaphoreType.DMA((devices,)),
            pltpu.SemaphoreType.DMA((dims, 6)),
            pltpu.SemaphoreType.DMA((dims, 6)),
            pltpu.SemaphoreType.DMA((dims, 4)),
            pltpu.SemaphoreType.DMA((dims, 4)),
        ],
        compiler_params=pltpu.CompilerParams(
            collective_id=0, has_side_effects=True, vmem_limit_bytes=60 << 20
        ),
        cost_estimate=pl.CostEstimate(
            flops=20 * 10**9, bytes_accessed=45 * 10**6, transcendentals=10**6
        ),
    )(tokens, router_t, numbers, pages, w_in, w_out)


def page_places(rows, page_cap):
    row = lax.broadcasted_iota(jnp.int32, (rows, 128), 0)
    within = lax.rem(row, 16)
    return lax.div(row, 16), lax.div(within, page_cap), lax.rem(within, page_cap)


def pack_kernel(page_cap, pages_here, slot_ref, routes_ref, cache_ref, pages_ref, numbers_ref,
                slot_row, stacked):
    me = lax.axis_index("row") * lax.axis_size("col") + lax.axis_index("col")
    rows, part_width = pages_ref.shape
    parts = 16 // page_cap
    page_width = cache_ref.shape[1]
    top_count, tok_count = routes_ref.shape
    numbers_ref[...] = jnp.zeros_like(numbers_ref)
    group = 128 // tok_count
    for i in range(group):
        numbers_ref[:top_count, i * tok_count : (i + 1) * tok_count] = jnp.where(
            me % group == i, routes_ref[...], 0
        )
    numbers_ref[top_count : top_count + 1, :pages_here] = slot_ref[...]
    slot_row[...] = jnp.zeros_like(slot_row)
    slot_row[:, :pages_here] = slot_ref[...]
    target = lax.div(slot_row[...], pages_here)
    across = jnp.broadcast_to(target.astype(jnp.float32), (128, 128))
    upper = lax.broadcasted_iota(jnp.int32, (128, 128), 0) < lax.broadcasted_iota(
        jnp.int32, (128, 128), 1
    )
    same = (across.T == across) & upper
    rank = jnp.sum(jnp.where(same, 1.0, 0.0), axis=0, keepdims=True).astype(jnp.int32)
    live = lax.broadcasted_iota(jnp.int32, (1, 128), 1) < pages_here
    placed = jnp.where(live, target * page_cap + rank, -1)
    dest, part_of, nth = page_places(rows, page_cap)
    match = (dest * page_cap + nth) == placed
    stacked[...] = jnp.zeros_like(stacked)
    picks = []
    for p in range(parts):
        size = min(part_width, page_width - p * part_width)
        stacked[p * 128 : p * 128 + pages_here, :size] = cache_ref[
            :, p * part_width : p * part_width + size
        ]
        picks.append(jnp.where(match & (part_of == p), 1.0, 0.0).astype(jnp.bfloat16))
    pages_ref[...] = jnp.dot(
        jnp.concatenate(picks, axis=1), stacked[...], preferred_element_type=jnp.float32
    ).astype(jnp.bfloat16)


def place_kernel(page_cap, top_count, numbers_ref, arrived_ref, out_ref):
    me = lax.axis_index("row") * lax.axis_size("col") + lax.axis_index("col")
    rows, part_width = arrived_ref.shape
    pages_here, page_width = out_ref.shape
    slots = numbers_ref[:, top_count, :]
    slots = jnp.broadcast_to(slots[:, None, :], (rows // 16, 16, 128)).reshape(rows, 128)
    lane = lax.broadcasted_iota(jnp.int32, (rows, 128), 1)
    mine = (lax.div(slots, pages_here) == me) & (lane < pages_here)
    earlier = lax.broadcasted_iota(jnp.int32, (128, 128), 0) < lax.broadcasted_iota(
        jnp.int32, (128, 128), 1
    )
    rank = jnp.dot(
        jnp.where(mine, 1.0, 0.0).astype(jnp.bfloat16),
        jnp.where(earlier, 1.0, 0.0).astype(jnp.bfloat16),
        preferred_element_type=jnp.float32,
    )
    _, part_of, nth = page_places(rows, page_cap)
    taken = mine & (rank == nth.astype(jnp.float32))
    within = lax.rem(slots, pages_here).astype(jnp.float32) + 1.0
    landing = jnp.sum(jnp.where(taken, within, 0.0), axis=1, keepdims=True) - 1.0
    match = landing == lane.astype(jnp.float32)
    for p in range(16 // page_cap):
        size = min(part_width, page_width - p * part_width)
        pick = jnp.where(match & (part_of == p), 1.0, 0.0).astype(jnp.bfloat16)
        out_ref[:, p * part_width : p * part_width + size] = lax.dot_general(
            pick, arrived_ref[:, :size], (((0,), (0,)), ((), ())),
            preferred_element_type=jnp.float32,
        )[:pages_here].astype(jnp.bfloat16)


def pack_pages(page_slot, routes, cache_prefill, devices, page_cap):
    pages_here, page_width = cache_prefill.shape
    parts = 16 // page_cap
    part_width = -(-page_width // (parts * 128)) * 128
    rows = devices * 16
    return pl.pallas_call(
        functools.partial(pack_kernel, page_cap, pages_here),
        in_specs=[pl.BlockSpec(memory_space=pltpu.VMEM)] * 3,
        out_specs=[pl.BlockSpec(memory_space=pltpu.VMEM)] * 2,
        out_shape=[
            jax.ShapeDtypeStruct((rows, part_width), jnp.bfloat16),
            jax.ShapeDtypeStruct((8, 128), jnp.int32),
        ],
        scratch_shapes=[
            pltpu.VMEM((1, 128), jnp.int32),
            pltpu.VMEM((parts * 128, part_width), jnp.bfloat16),
        ],
        compiler_params=pltpu.CompilerParams(vmem_limit_bytes=48 << 20),
    )(page_slot[None], routes.T, cache_prefill)


def place_pages(numbers, arrived, shape, page_cap, top_count):
    return pl.pallas_call(
        functools.partial(place_kernel, page_cap, top_count),
        in_specs=[pl.BlockSpec(memory_space=pltpu.VMEM)] * 2,
        out_specs=pl.BlockSpec(memory_space=pltpu.VMEM),
        out_shape=jax.ShapeDtypeStruct(shape, jnp.bfloat16),
        compiler_params=pltpu.CompilerParams(vmem_limit_bytes=48 << 20),
    )(numbers, arrived)


def per_device(tokens, routes, router, w_in, w_out, cache_prefill, page_slot):
    devices = lax.axis_size(AXES)
    me = lax.axis_index(AXES)
    pages_here, page_width = cache_prefill.shape
    page_cap = pages_here // devices + 1
    tok_count, top_count = routes.shape
    halves_here = w_in.shape[0]

    if devices * tok_count <= FUSED_TOKENS and tok_count * 4 <= 128 and pages_here <= 128:
        pages, block = pack_pages(page_slot, routes, cache_prefill, devices, page_cap)
        moe_out, arrived, numbers = run_fused(
            lax.axis_size("row"), lax.axis_size("col"), tokens, router.T, block,
            pages.reshape(devices, 16, -1), w_in, w_out,
        )
        cache_decode = place_pages(
            numbers.reshape(devices, 8, 128), arrived.reshape(pages.shape),
            cache_prefill.shape, page_cap, top_count,
        )
        return moe_out, cache_decode

    target = page_slot // pages_here
    same = target[:, None] == target[None, :]
    earlier = jnp.arange(pages_here)[None, :] < jnp.arange(pages_here)[:, None]
    placed = target * page_cap + jnp.sum((same & earlier).astype(jnp.int32), axis=1)
    send_pick = (jnp.arange(devices * page_cap)[:, None] == placed[None, :]).astype(jnp.bfloat16)
    outgoing = jnp.dot(send_pick, cache_prefill, preferred_element_type=jnp.float32).astype(
        jnp.bfloat16
    )
    arrived = lax.all_to_all(outgoing, AXES, split_axis=0, concat_axis=0, tiled=True)

    numbers = jnp.concatenate([routes.reshape(-1), page_slot])
    numbers = lax.all_gather(numbers[None], AXES, axis=0, tiled=True)
    x = lax.all_gather(tokens, AXES, axis=0, tiled=True)
    all_routes = numbers[:, : tok_count * top_count].reshape(devices * tok_count, top_count)
    base = jnp.reshape((me * halves_here) % EXPERTS, (1,)).astype(jnp.int32)
    partial = run_experts(base, x, router.T, all_routes.T, w_in, w_out, devices)
    moe_out = lax.psum_scatter(partial, AXES, scatter_dimension=0, tiled=True)
    slots = numbers[:, tok_count * top_count :]

    mine = slots // pages_here == me
    order = jnp.sum((mine[:, None, :] & earlier[None]).astype(jnp.int32), axis=2)
    taken = mine[:, None, :] & (order[:, None, :] == jnp.arange(page_cap)[None, :, None])
    landing = jnp.sum(jnp.where(taken, slots[:, None, :] % pages_here + 1, 0), axis=2) - 1
    land_pick = (jnp.arange(pages_here)[:, None] == landing.reshape(1, -1)).astype(jnp.bfloat16)
    cache_decode = jnp.dot(land_pick, arrived, preferred_element_type=jnp.float32).astype(
        jnp.bfloat16
    )
    return moe_out, cache_decode


def solution(mesh):
    in_specs = (
        P(AXES, None),
        P(AXES, None),
        P(),
        P(AXES, None, None),
        P(AXES, None, None),
        P(AXES, None),
        P(AXES),
    )
    out_specs = (P(AXES, None), P(AXES, None))
    return jax.shard_map(
        per_device, mesh=mesh, in_specs=in_specs, out_specs=out_specs, check_vma=False
    )
```

```python
import functools

import jax
import jax.numpy as jnp
from jax import lax
from jax.experimental import pallas as pl
from jax.experimental.pallas import tpu as pltpu
from jax.sharding import PartitionSpec as P

EXPERTS = 64
CAPE = 6
AXES = ("row", "col")
ROUTE_SCALE = 2.446
CHUNK = 512
TOP = 6
MESH = pl.DeviceIdType.MESH
FUSED_TOKENS = 1024


def experts_kernel(base_ref, x_ref, router_ref, routes_ref, w_in_ref, w_out_ref, out_ref,
                   gates, ranks, weighted):
    step = pl.program_id(0)
    steps = pl.num_programs(0)
    count = x_ref.shape[0]
    rows = weighted.shape[1]
    hidden = w_out_ref.shape[1]

    @pl.when(step == 0)
    def _():
        expert_row = lax.broadcasted_iota(jnp.int32, (EXPERTS, CHUNK), 0)
        earlier = (
            lax.broadcasted_iota(jnp.int32, (CHUNK, CHUNK), 0)
            < lax.broadcasted_iota(jnp.int32, (CHUNK, CHUNK), 1)
        ).astype(jnp.float32).astype(jnp.bfloat16)
        offset = jnp.zeros((EXPERTS, 1), jnp.float32)
        for begin in range(0, count, CHUNK):
            part = slice(begin, begin + CHUNK)
            logits = lax.dot_general(
                router_ref[...], x_ref[part, :], (((1,), (1,)), ((), ())),
                preferred_element_type=jnp.float32,
            )
            scores = 1.0 / (1.0 + jnp.exp(-logits))
            named = jnp.zeros((EXPERTS, CHUNK), jnp.float32)
            for k in range(routes_ref.shape[0]):
                named = jnp.where(routes_ref[k : k + 1, part] == expert_row, 1.0, named)
            picked = scores * named
            gates[:, part] = ROUTE_SCALE * picked / jnp.sum(picked, axis=0, keepdims=True)
            before = offset + jnp.dot(
                named.astype(jnp.bfloat16), earlier, preferred_element_type=jnp.float32
            )
            ranks[:, part] = jnp.where(named > 0.0, before, -1.0)
            offset = offset + jnp.sum(named, axis=1, keepdims=True)

    expert = base_ref[0] + step

    def chosen(which, part):
        slots = lax.broadcasted_iota(jnp.int32, (rows, part.size), 0).astype(jnp.float32)
        return ranks[pl.ds(which, 1), part] == slots

    picked_rows = jnp.zeros((rows, x_ref.shape[1]), jnp.float32)
    row_gate = jnp.zeros((rows, 1), jnp.float32)
    for begin in range(0, count, CHUNK):
        part = pl.ds(begin, CHUNK)
        hit = chosen(expert, part)
        picked_rows += jnp.dot(
            hit.astype(jnp.float32).astype(jnp.bfloat16), x_ref[part, :],
            preferred_element_type=jnp.float32,
        )
        row_gate += jnp.sum(
            jnp.where(hit, gates[pl.ds(expert, 1), part], 0.0), axis=1, keepdims=True
        )
    gate_up = jnp.dot(
        picked_rows.astype(jnp.bfloat16), w_in_ref[0], preferred_element_type=jnp.float32
    )
    gate = gate_up[:, :hidden]
    activated = (gate / (1.0 + jnp.exp(-gate)) * gate_up[:, hidden:]).astype(jnp.bfloat16)
    half = jnp.dot(activated, w_out_ref[0], preferred_element_type=jnp.float32)
    weighted[pl.ds(step, 1)] = (half * row_gate).astype(jnp.bfloat16)[None]

    @pl.when(step == steps - 1)
    def _():
        for begin in range(0, count, CHUNK):
            part = pl.ds(begin, CHUNK)
            hits = jnp.concatenate(
                [
                    chosen(base_ref[0] + j, part).astype(jnp.float32).astype(jnp.bfloat16)
                    for j in range(weighted.shape[0])
                ],
                axis=0,
            )
            out_ref[part, :] = lax.dot_general(
                hits, weighted[...].reshape(-1, weighted.shape[2]),
                (((0,), (0,)), ((), ())), preferred_element_type=jnp.float32,
            ).astype(jnp.bfloat16)


def run_experts(base, x, router_t, routes_t, w_in, w_out, devices):
    count, width = x.shape
    halves_here, hidden, _ = w_out.shape
    rows = CAPE * devices
    whole = functools.partial(pl.BlockSpec, pipeline_mode=pl.Buffered(1))
    return pl.pallas_call(
        experts_kernel,
        grid=(halves_here,),
        in_specs=[
            pl.BlockSpec(memory_space=pltpu.SMEM),
            whole((count, width), lambda j: (0, 0)),
            whole(router_t.shape, lambda j: (0, 0)),
            whole(routes_t.shape, lambda j: (0, 0)),
            pl.BlockSpec((1,) + w_in.shape[1:], lambda j: (j, 0, 0)),
            pl.BlockSpec((1,) + w_out.shape[1:], lambda j: (j, 0, 0)),
        ],
        out_specs=whole((count, width), lambda j: (0, 0)),
        out_shape=jax.ShapeDtypeStruct((count, width), jnp.bfloat16),
        scratch_shapes=[
            pltpu.VMEM((EXPERTS, count), jnp.float32),
            pltpu.VMEM((EXPERTS, count), jnp.float32),
            pltpu.VMEM((halves_here, rows, width), jnp.bfloat16),
        ],
        compiler_params=pltpu.CompilerParams(vmem_limit_bytes=60 << 20),
        cost_estimate=pl.CostEstimate(
            flops=20 * 10**9, bytes_accessed=45 * 10**6, transcendentals=10**6
        ),
    )(base, x, router_t, routes_t, w_in, w_out)


def bits_of(number, count):
    return [(number // 2 ** (count - 1 - b)) % 2 for b in range(count)]


def fused_kernel(n_row, n_col, tokens_ref, router_ref, numbers_ref, pages_ref, w_in_hbm, w_out_hbm,
                 out_ref, arrived_ref, all_numbers_ref,
                 x, part, gates, ranks, weighted, activated, row_gates, w_in_buf, w_out_buf, *rest):
    devices = n_row * n_col
    dims = devices.bit_length() - 1
    row_bits = n_row.bit_length() - 1
    sends, receives = rest[:dims], rest[dims : 2 * dims]
    (w_sem, v_sem, own_sem, page_send, page_recv, gather_send, gather_recv,
     sum_send, sum_recv) = rest[2 * dims :]
    row, col = lax.axis_index("row"), lax.axis_index("col")
    me = row * n_col + col
    mine = bits_of(me, dims)
    tok_count, width = tokens_ref.shape
    halves_here, hidden, _ = w_out_hbm.shape
    rows = weighted.shape[1]
    split = width // 4
    columns = [pl.ds(c * split, split) for c in range(4)]
    inner = list(range(row_bits, dims - 1))
    orders = [
        list(range(row_bits)) + inner + [dims - 1],
        list(range(row_bits)) + inner[::-1] + [dims - 1],
    ]

    def place(number):
        return (number // n_col, number % n_col)

    def partner(b):
        return place(me + (1 - 2 * mine[b]) * 2 ** (dims - 1 - b))

    slots = w_in_buf.shape[0]

    def first_weights(j):
        slot = j % slots
        return pltpu.make_async_copy(w_in_hbm.at[j], w_in_buf.at[slot], w_sem.at[slot])

    def second_weights(j):
        return pltpu.make_async_copy(w_out_hbm.at[j], w_out_buf.at[j], v_sem.at[j])

    for j in range(slots):
        first_weights(j).start()
    for j in range(halves_here):
        second_weights(j).start()
    own = pltpu.make_async_copy(pages_ref.at[me], arrived_ref.at[me], own_sem)
    own.start()

    barrier = pltpu.get_barrier_semaphore()

    @pl.loop(1, devices)
    def _(o):
        pl.semaphore_signal(barrier, inc=1, device_id=place((me + o) % devices), device_id_type=MESH)

    x[tuple(mine)] = tokens_ref[...]
    all_numbers_ref[tuple(mine)] = numbers_ref[...]
    pl.semaphore_wait(barrier, devices - 1)

    def page(o):
        to = (me + o) % devices
        return pltpu.make_async_remote_copy(
            src_ref=pages_ref.at[to], dst_ref=arrived_ref.at[me],
            send_sem=page_send.at[o], recv_sem=page_recv.at[o],
            device_id=place(to), device_id_type=MESH,
        )

    def start_page(to_row, to_col):
        page((to_row * n_col + to_col - me + devices) % devices).start()

    def gather(g, s):
        copies = []
        for h in range(3 - g):
            order = orders[h % 2]
            done, b = order[:s], order[s]
            index = tuple(slice(None) if d in done else mine[d] for d in range(dims))
            if h < 2:
                ref = x.at[index + (slice(None), columns[2 * g + h])]
            else:
                ref = all_numbers_ref.at[index]
            copies.append(
                pltpu.make_async_remote_copy(
                    src_ref=ref, dst_ref=ref,
                    send_sem=gather_send.at[s, 2 * h + g], recv_sem=gather_recv.at[s, 2 * h + g],
                    device_id=partner(b), device_id_type=MESH,
                )
            )
        return copies

    for tick in range(dims + 1):
        for g in range(2):
            s = tick - g
            if 0 < s <= dims:
                for copy in gather(g, s - 1):
                    copy.wait()
            if 0 <= s < dims:
                for copy in gather(g, s):
                    copy.start()
        if tick == 0:

            @pl.loop(1, n_col)
            def _(i):
                start_page(row, (col + i) % n_col)

        if tick == row_bits:

            @pl.loop(0, 2 * (n_row - 1))
            def _(i):
                start_page((row + 1 + i // 2) % n_row, col // 2 * 2 + i % 2)

    @pl.loop(0, (n_row - 1) * (n_col - 2))
    def _(i):
        start_page(
            (row + 1 + i % (n_row - 1)) % n_row,
            (col // 2 * 2 + 2 + i // (n_row - 1)) % n_col,
        )

    for copy in gather(1, dims - 1):
        copy.wait()

    chunk = devices // 2 * tok_count
    group = 128 // tok_count

    def tokens_of(q):
        return x[q].reshape(chunk, width)

    expert_row = lax.broadcasted_iota(jnp.int32, (EXPERTS, chunk), 0)
    earlier = (
        lax.broadcasted_iota(jnp.int32, (chunk, chunk), 0)
        < lax.broadcasted_iota(jnp.int32, (chunk, chunk), 1)
    ).astype(jnp.float32).astype(jnp.bfloat16)
    offset = jnp.zeros((EXPERTS, 1), jnp.float32)
    for q in range(2):
        part_q = slice(q * chunk, (q + 1) * chunk)
        numbers = all_numbers_ref[q].reshape(-1, group, 8, 128)
        numbers = [
            functools.reduce(lambda a, b: a + b, [numbers[i, g] for g in range(group)])
            for i in range(numbers.shape[0])
        ]
        routes = jnp.concatenate(numbers, axis=1)
        logits = lax.dot_general(
            router_ref[...], tokens_of(q), (((1,), (1,)), ((), ())),
            preferred_element_type=jnp.float32,
        )
        scores = 1.0 / (1.0 + jnp.exp(-logits))
        named = jnp.zeros((EXPERTS, chunk), jnp.float32)
        for k in range(TOP):
            named = jnp.where(routes[k : k + 1, :] == expert_row, 1.0, named)
        picked = scores * named
        gates[:, part_q] = ROUTE_SCALE * picked / jnp.sum(picked, axis=0, keepdims=True)
        before = offset + jnp.dot(
            named.astype(jnp.bfloat16), earlier, preferred_element_type=jnp.float32
        )
        ranks[:, part_q] = jnp.where(named > 0.0, before, -1.0)
        offset = offset + jnp.sum(named, axis=1, keepdims=True)

    base = (me * halves_here) % EXPERTS

    def chosen(which, q):
        numbering = lax.broadcasted_iota(jnp.int32, (rows, chunk), 0).astype(jnp.float32)
        return ranks[pl.ds(which, 1), q * chunk : (q + 1) * chunk] == numbering

    @pl.loop(0, halves_here)
    def _(j):
        expert = base + j
        picked_rows = jnp.zeros((rows, width), jnp.float32)
        row_gate = jnp.zeros((rows, 1), jnp.float32)
        for q in range(2):
            hit = chosen(expert, q)
            picked_rows += jnp.dot(
                hit.astype(jnp.float32).astype(jnp.bfloat16), tokens_of(q),
                preferred_element_type=jnp.float32,
            )
            row_gate += jnp.sum(
                jnp.where(hit, gates[pl.ds(expert, 1), q * chunk : (q + 1) * chunk], 0.0),
                axis=1, keepdims=True,
            )
        row_gates[pl.ds(j, 1)] = row_gate[None]
        first_weights(j).wait()
        gate_up = jnp.dot(
            picked_rows.astype(jnp.bfloat16), w_in_buf[j % slots],
            preferred_element_type=jnp.float32,
        )
        gate = gate_up[:, :hidden]
        activated[pl.ds(j, 1)] = (
            gate / (1.0 + jnp.exp(-gate)) * gate_up[:, hidden:]
        ).astype(jnp.bfloat16)[None]

        @pl.when(j + slots < halves_here)
        def _():
            first_weights(j + slots).start()

    for j in range(halves_here):
        second_weights(j).wait()

    def sum_experts(g):
        begin, size = 2 * g * split, 2 * split
        for j in range(halves_here):
            half = jnp.dot(
                activated[j], w_out_buf[j, :, begin : begin + size],
                preferred_element_type=jnp.float32,
            )
            weighted[j, :, begin : begin + size] = (half * row_gates[j]).astype(jnp.bfloat16)
        for q in range(2):
            hits = jnp.concatenate(
                [
                    chosen(base + j, q).astype(jnp.float32).astype(jnp.bfloat16)
                    for j in range(halves_here)
                ],
                axis=0,
            )
            part[pl.ds(q * (devices // 2), devices // 2), :, pl.ds(begin, size)] = lax.dot_general(
                hits, weighted[:, :, begin : begin + size].reshape(halves_here * rows, size),
                (((0,), (0,)), ((), ())), preferred_element_type=jnp.float32,
            ).reshape(devices // 2, tok_count, size)

    def blocks(order, s, flip):
        fixed = {b: mine[b] for b in order[:s]}
        fixed[order[s]] = 1 - mine[order[s]] if flip else mine[order[s]]
        free = sorted(order[s + 1 :])
        for i in range(2 ** len(free)):
            bits = dict(fixed)
            for place_of, d in enumerate(free):
                bits[d] = (i >> (len(free) - 1 - place_of)) & 1
            yield i, sum(bits[d] * 2 ** (dims - 1 - d) for d in range(dims))

    def sum_copy(g, s, h):
        cols = columns[2 * g + h]
        return pltpu.make_async_remote_copy(
            src_ref=sends[s].at[:, :, cols], dst_ref=receives[s].at[:, :, cols],
            send_sem=sum_send.at[s, 2 * h + g], recv_sem=sum_recv.at[s, 2 * h + g],
            device_id=partner(orders[h][dims - 1 - s]), device_id_type=MESH,
        )

    def sum_start(g, s):
        for h in range(2):
            cols = columns[2 * g + h]
            for i, block in blocks(orders[h][::-1], s, True):
                sends[s][i, :, cols] = part[block, :, cols].astype(jnp.bfloat16)
            sum_copy(g, s, h).start()

    def sum_finish(g, s):
        for h in range(2):
            cols = columns[2 * g + h]
            sum_copy(g, s, h).wait()
            for i, block in blocks(orders[h][::-1], s, False):
                part[block, :, cols] += receives[s][i, :, cols].astype(jnp.float32)

    sum_experts(0)
    sum_start(0, 0)
    sum_experts(1)
    for tick in range(1, dims + 2):
        for g in range(2):
            s = tick - g
            if 0 < s <= dims:
                sum_finish(g, s - 1)
            if 0 <= s < dims:
                sum_start(g, s)
    out_ref[...] = part[me].astype(jnp.bfloat16)

    own.wait()

    @pl.loop(1, devices)
    def _(o):
        page(o).wait()


def run_fused(n_row, n_col, tokens, router_t, numbers, pages, w_in, w_out):
    devices = n_row * n_col
    dims = devices.bit_length() - 1
    tok_count, width = tokens.shape
    halves_here, hidden, _ = w_out.shape
    count = devices * tok_count
    rows = CAPE * devices
    cube = (2,) * dims
    slots = min(3, halves_here)
    vmem = pl.BlockSpec(memory_space=pltpu.VMEM)
    anywhere = pl.BlockSpec(memory_space=pl.ANY)
    parts = [pltpu.VMEM((2 ** (dims - 1 - s), tok_count, width), jnp.bfloat16) for s in range(dims)]
    return pl.pallas_call(
        functools.partial(fused_kernel, n_row, n_col),
        in_specs=[vmem, vmem, vmem, anywhere, anywhere, anywhere],
        out_specs=[vmem, anywhere, vmem],
        out_shape=[
            jax.ShapeDtypeStruct((tok_count, width), jnp.bfloat16),
            jax.ShapeDtypeStruct(pages.shape, jnp.bfloat16),
            jax.ShapeDtypeStruct(cube + numbers.shape, jnp.int32),
        ],
        scratch_shapes=[
            pltpu.VMEM(cube + (tok_count, width), jnp.bfloat16),
            pltpu.VMEM((devices, tok_count, width), jnp.float32),
            pltpu.VMEM((EXPERTS, count), jnp.float32),
            pltpu.VMEM((EXPERTS, count), jnp.float32),
            pltpu.VMEM((halves_here, rows, width), jnp.bfloat16),
            pltpu.VMEM((halves_here, rows, hidden), jnp.bfloat16),
            pltpu.VMEM((halves_here, rows, 1), jnp.float32),
            pltpu.VMEM((slots,) + w_in.shape[1:], jnp.bfloat16),
            pltpu.VMEM(w_out.shape, jnp.bfloat16),
            *parts,
            *parts,
            pltpu.SemaphoreType.DMA((slots,)),
            pltpu.SemaphoreType.DMA((halves_here,)),
            pltpu.SemaphoreType.DMA(()),
            pltpu.SemaphoreType.DMA((devices,)),
            pltpu.SemaphoreType.DMA((devices,)),
            pltpu.SemaphoreType.DMA((dims, 6)),
            pltpu.SemaphoreType.DMA((dims, 6)),
            pltpu.SemaphoreType.DMA((dims, 4)),
            pltpu.SemaphoreType.DMA((dims, 4)),
        ],
        compiler_params=pltpu.CompilerParams(
            collective_id=0, has_side_effects=True, vmem_limit_bytes=60 << 20
        ),
        cost_estimate=pl.CostEstimate(
            flops=20 * 10**9, bytes_accessed=45 * 10**6, transcendentals=10**6
        ),
    )(tokens, router_t, numbers, pages, w_in, w_out)


def page_places(rows, page_cap):
    row = lax.broadcasted_iota(jnp.int32, (rows, 128), 0)
    within = lax.rem(row, 16)
    return lax.div(row, 16), lax.div(within, page_cap), lax.rem(within, page_cap)


def pack_kernel(page_cap, pages_here, slot_ref, routes_ref, cache_ref, pages_ref, numbers_ref,
                slot_row, stacked):
    me = lax.axis_index("row") * lax.axis_size("col") + lax.axis_index("col")
    rows, part_width = pages_ref.shape
    parts = 16 // page_cap
    page_width = cache_ref.shape[1]
    top_count, tok_count = routes_ref.shape
    numbers_ref[...] = jnp.zeros_like(numbers_ref)
    group = 128 // tok_count
    for i in range(group):
        numbers_ref[:top_count, i * tok_count : (i + 1) * tok_count] = jnp.where(
            me % group == i, routes_ref[...], 0
        )
    numbers_ref[top_count : top_count + 1, :pages_here] = slot_ref[...]
    slot_row[...] = jnp.zeros_like(slot_row)
    slot_row[:, :pages_here] = slot_ref[...]
    target = lax.div(slot_row[...], pages_here)
    across = jnp.broadcast_to(target.astype(jnp.float32), (128, 128))
    upper = lax.broadcasted_iota(jnp.int32, (128, 128), 0) < lax.broadcasted_iota(
        jnp.int32, (128, 128), 1
    )
    same = (across.T == across) & upper
    rank = jnp.sum(jnp.where(same, 1.0, 0.0), axis=0, keepdims=True).astype(jnp.int32)
    live = lax.broadcasted_iota(jnp.int32, (1, 128), 1) < pages_here
    placed = jnp.where(live, target * page_cap + rank, -1)
    dest, part_of, nth = page_places(rows, page_cap)
    match = (dest * page_cap + nth) == placed
    stacked[...] = jnp.zeros_like(stacked)
    picks = []
    for p in range(parts):
        size = min(part_width, page_width - p * part_width)
        stacked[p * 128 : p * 128 + pages_here, :size] = cache_ref[
            :, p * part_width : p * part_width + size
        ]
        picks.append(jnp.where(match & (part_of == p), 1.0, 0.0).astype(jnp.bfloat16))
    pages_ref[...] = jnp.dot(
        jnp.concatenate(picks, axis=1), stacked[...], preferred_element_type=jnp.float32
    ).astype(jnp.bfloat16)


def place_kernel(page_cap, top_count, numbers_ref, arrived_ref, out_ref):
    me = lax.axis_index("row") * lax.axis_size("col") + lax.axis_index("col")
    rows, part_width = arrived_ref.shape
    pages_here, page_width = out_ref.shape
    slots = numbers_ref[:, top_count, :]
    slots = jnp.broadcast_to(slots[:, None, :], (rows // 16, 16, 128)).reshape(rows, 128)
    lane = lax.broadcasted_iota(jnp.int32, (rows, 128), 1)
    mine = (lax.div(slots, pages_here) == me) & (lane < pages_here)
    earlier = lax.broadcasted_iota(jnp.int32, (128, 128), 0) < lax.broadcasted_iota(
        jnp.int32, (128, 128), 1
    )
    rank = jnp.dot(
        jnp.where(mine, 1.0, 0.0).astype(jnp.bfloat16),
        jnp.where(earlier, 1.0, 0.0).astype(jnp.bfloat16),
        preferred_element_type=jnp.float32,
    )
    _, part_of, nth = page_places(rows, page_cap)
    taken = mine & (rank == nth.astype(jnp.float32))
    within = lax.rem(slots, pages_here).astype(jnp.float32) + 1.0
    landing = jnp.sum(jnp.where(taken, within, 0.0), axis=1, keepdims=True) - 1.0
    match = landing == lane.astype(jnp.float32)
    for p in range(16 // page_cap):
        size = min(part_width, page_width - p * part_width)
        pick = jnp.where(match & (part_of == p), 1.0, 0.0).astype(jnp.bfloat16)
        out_ref[:, p * part_width : p * part_width + size] = lax.dot_general(
            pick, arrived_ref[:, :size], (((0,), (0,)), ((), ())),
            preferred_element_type=jnp.float32,
        )[:pages_here].astype(jnp.bfloat16)


def pack_pages(page_slot, routes, cache_prefill, devices, page_cap):
    pages_here, page_width = cache_prefill.shape
    parts = 16 // page_cap
    part_width = -(-page_width // (parts * 128)) * 128
    rows = devices * 16
    return pl.pallas_call(
        functools.partial(pack_kernel, page_cap, pages_here),
        in_specs=[pl.BlockSpec(memory_space=pltpu.VMEM)] * 3,
        out_specs=[pl.BlockSpec(memory_space=pltpu.VMEM)] * 2,
        out_shape=[
            jax.ShapeDtypeStruct((rows, part_width), jnp.bfloat16),
            jax.ShapeDtypeStruct((8, 128), jnp.int32),
        ],
        scratch_shapes=[
            pltpu.VMEM((1, 128), jnp.int32),
            pltpu.VMEM((parts * 128, part_width), jnp.bfloat16),
        ],
        compiler_params=pltpu.CompilerParams(vmem_limit_bytes=48 << 20),
    )(page_slot[None], routes.T, cache_prefill)


def place_pages(numbers, arrived, shape, page_cap, top_count):
    return pl.pallas_call(
        functools.partial(place_kernel, page_cap, top_count),
        in_specs=[pl.BlockSpec(memory_space=pltpu.VMEM)] * 2,
        out_specs=pl.BlockSpec(memory_space=pltpu.VMEM),
        out_shape=jax.ShapeDtypeStruct(shape, jnp.bfloat16),
        compiler_params=pltpu.CompilerParams(vmem_limit_bytes=48 << 20),
    )(numbers, arrived)


def per_device(tokens, routes, router, w_in, w_out, cache_prefill, page_slot):
    devices = lax.axis_size(AXES)
    me = lax.axis_index(AXES)
    pages_here, page_width = cache_prefill.shape
    page_cap = pages_here // devices + 1
    tok_count, top_count = routes.shape
    halves_here = w_in.shape[0]

    if devices * tok_count <= FUSED_TOKENS and tok_count * 4 <= 128 and pages_here <= 128:
        pages, block = pack_pages(page_slot, routes, cache_prefill, devices, page_cap)
        moe_out, arrived, numbers = run_fused(
            lax.axis_size("row"), lax.axis_size("col"), tokens, router.T, block,
            pages.reshape(devices, 16, -1), w_in, w_out,
        )
        cache_decode = place_pages(
            numbers.reshape(devices, 8, 128), arrived.reshape(pages.shape),
            cache_prefill.shape, page_cap, top_count,
        )
        return moe_out, cache_decode

    target = page_slot // pages_here
    same = target[:, None] == target[None, :]
    earlier = jnp.arange(pages_here)[None, :] < jnp.arange(pages_here)[:, None]
    placed = target * page_cap + jnp.sum((same & earlier).astype(jnp.int32), axis=1)
    send_pick = (jnp.arange(devices * page_cap)[:, None] == placed[None, :]).astype(jnp.bfloat16)
    outgoing = jnp.dot(send_pick, cache_prefill, preferred_element_type=jnp.float32).astype(
        jnp.bfloat16
    )
    arrived = lax.all_to_all(outgoing, AXES, split_axis=0, concat_axis=0, tiled=True)

    numbers = jnp.concatenate([routes.reshape(-1), page_slot])
    numbers = lax.all_gather(numbers[None], AXES, axis=0, tiled=True)
    x = lax.all_gather(tokens, AXES, axis=0, tiled=True)
    all_routes = numbers[:, : tok_count * top_count].reshape(devices * tok_count, top_count)
    base = jnp.reshape((me * halves_here) % EXPERTS, (1,)).astype(jnp.int32)
    partial = run_experts(base, x, router.T, all_routes.T, w_in, w_out, devices)
    moe_out = lax.psum_scatter(partial, AXES, scatter_dimension=0, tiled=True)
    slots = numbers[:, tok_count * top_count :]

    mine = slots // pages_here == me
    order = jnp.sum((mine[:, None, :] & earlier[None]).astype(jnp.int32), axis=2)
    taken = mine[:, None, :] & (order[:, None, :] == jnp.arange(page_cap)[None, :, None])
    landing = jnp.sum(jnp.where(taken, slots[:, None, :] % pages_here + 1, 0), axis=2) - 1
    land_pick = (jnp.arange(pages_here)[:, None] == landing.reshape(1, -1)).astype(jnp.bfloat16)
    cache_decode = jnp.dot(land_pick, arrived, preferred_element_type=jnp.float32).astype(
        jnp.bfloat16
    )
    return moe_out, cache_decode


def solution(mesh):
    in_specs = (
        P(AXES, None),
        P(AXES, None),
        P(),
        P(AXES, None, None),
        P(AXES, None, None),
        P(AXES, None),
        P(AXES),
    )
    out_specs = (P(AXES, None), P(AXES, None))
    return jax.shard_map(
        per_device, mesh=mesh, in_specs=in_specs, out_specs=out_specs, check_vma=False
    )
```
